256 devices in a mesh: row: 8 (over z), col: 16 (over y, x), rep: 2 (over core).
Axes of the slice: x: 4, y: 4, z: 8, core: 2. Of those that a mesh axis runs over, the one named last changes fastest.
Arguments:
- amplitudes: bfloat16 [4, 512, 16384], P(None, 'col', ('row', 'rep')), may hold values from -6 to 6
- ladder_integrals: bfloat16 [4, 16384, 16384], P(None, ('row', 'rep'), 'col'), may hold values from -0.046875 to 0.046875
- hole_integrals: bfloat16 [4, 512, 4, 512], P(None, ('row', 'rep'), None, 'col'), may hold values from -0.25 to 0.25
- denominators: float32 [4, 512, 16384], P(None, ('row', 'rep'), 'col'), may hold values from 1 to 10
- pair_irrep: int32 [4], replicated, may hold values from 0 to 7
- irrep_pairs: int32 [8], replicated, may hold values from 1 to 16384, 81920 in all
Outputs:
- update: bfloat16 [4, 512, 16384], P(None, ('row', 'rep'), 'col')
The draws below stay inside these ranges and needn't reach their ends.
Inputs may be any that keep to these rules, and one draw needn't show every extreme that they name: `irrep_pairs`: one irrep product has 16384 used virtual pairs.
All inputs are finite; a program needn't handle non-finite values.
Results may differ from the reference program's by a relative error of at most 0.001.
Values may be sent and summed in bfloat16 or wider, within the bound.
A program may use at most 128 MiB of HBM per device.

```python
import math
import jax
import jax.numpy as jnp
import numpy as np
from jax import lax

NIRR = 8
NQ = 4
PB = 512
NK = 16384


def with_ends(array, rng, smallest, largest):
    extent = array.shape
    place = [jax.random.randint(jax.random.fold_in(rng, axis), (), 0, extent[axis]) for axis in range(len(extent))]
    array = array.at[tuple(place)].set(smallest)
    longest = extent.index(max(extent))
    place[longest] = (place[longest] + 1) % extent[longest]
    return array.at[tuple(place)].set(largest)


def steps_of(rng, dims, cuts, least, high):
    level, own = 1.0, jax.random.fold_in(rng, 6)
    for dim, shards_of in cuts:
        draws = jnp.exp(jax.random.uniform(jax.random.fold_in(own, dim), (shards_of,), jnp.float32, least / len(cuts), high / len(cuts)))
        level = level * jnp.repeat(draws, dims[dim] // shards_of).reshape([-1 if axis == dim else 1 for axis in range(len(dims))])
    return level


def split_up(number_of, total, bound, lean):
    loads = [(1 << 20) // math.isqrt(rank ** lean) + 1 for rank in range(2, number_of + 1)]
    surplus, given = total - bound - (number_of - 1), [1] * (number_of - 1)
    while surplus > 0:
        free = [i for i in range(number_of - 1) if given[i] < bound]
        pool, remaining = sum([loads[i] for i in free]), surplus
        for i in free:
            addition = min(bound - given[i], max(1, remaining * loads[i] // pool), surplus)
            given[i] = given[i] + addition
            surplus = surplus - addition
    return np.array([bound] + given)


def uneven(own_key, count, total, most, slope):
    if count == 2:
        one = jax.random.randint(own_key, (), max(1, total - most), min(most, total - 1) + 1)
        return jnp.stack([one, total - one])
    lengths = jnp.asarray(split_up(count, total, most, slope), jnp.int32)
    couples = (count - 1) // 2
    donor, sink = lengths[1:1 + 2 * couples:2], lengths[2:2 + 2 * couples:2]
    margin = jnp.minimum(donor - 1, most - sink)
    passed = jax.random.randint(jax.random.fold_in(own_key, 1), (couples,), 0, 1 << 20) % (margin + 1)
    lengths = lengths.at[1:1 + 2 * couples:2].set(donor - passed).at[2:2 + 2 * couples:2].set(sink + passed)
    return lengths[jax.random.permutation(jax.random.fold_in(own_key, 2), count)]


def noise(rng, extent, width, limit, shards=(), kind=jnp.bfloat16):
    loudness = steps_of(rng, extent, shards, -0.22, 0.18) if shards else 1.0
    drawn = jax.random.normal(rng, extent, jnp.float32) * width * loudness
    return jnp.minimum(jnp.maximum(drawn, -limit), limit).astype(kind)


def setup_inputs(seed: int = 0) -> dict:
    arg_keys = jax.random.split(jax.random.key(seed), 7)
    amplitudes = noise(arg_keys[0], (NQ, PB, NK), 1.0, 6.0, ((1, 16), (2, 16)))
    ladder_integrals = noise(arg_keys[1], (NQ, NK, NK), NK ** -0.5, 0.046875, ((1, 16), (2, 16)))
    hole_integrals = noise(arg_keys[2], (NQ, PB, NQ, PB), PB ** -0.5, 0.25, ((1, 16), (3, 16)))
    denominators = jnp.clip(jnp.exp(math.log(10.0) - 2.3025851 * jax.random.uniform(arg_keys[3], (NQ, PB, NK), jnp.float32) ** steps_of(arg_keys[3], (NQ, PB, NK), ((1, 16), (2, 16)), -0.2, 0.2)), 1.0, 10.0)
    pair_irrep = with_ends(jax.random.randint(arg_keys[4], (NQ,), 0, NIRR), jax.random.fold_in(arg_keys[4], 1), 0, NIRR - 1).astype(jnp.int32)
    irrep_pairs = uneven(arg_keys[5], NIRR, NIRR * NK * 5 // 8, NK, 2).astype(jnp.int32)
    return {"amplitudes": amplitudes, "ladder_integrals": ladder_integrals, "hole_integrals": hole_integrals, "denominators": denominators, "pair_irrep": pair_irrep, "irrep_pairs": irrep_pairs}


def reference(amplitudes, ladder_integrals, hole_integrals, denominators, pair_irrep, irrep_pairs):
    limits = irrep_pairs[pair_irrep]
    columns = jnp.arange(NK, dtype=jnp.int32)
    valid = columns[None, :] < limits[:, None]
    masked = jnp.where(valid[:, None, :], amplitudes, jnp.zeros_like(amplitudes))
    alike = pair_irrep[:, None] == pair_irrep[None, :]
    stacked = masked.reshape(NQ * PB, NK)

    def block_update(block_id):
        integral = ladder_integrals[block_id]
        ladder = jnp.dot(masked[block_id], integral, preferred_element_type=jnp.float32)
        weights = jnp.where(alike[block_id][None, :, None], hole_integrals[block_id], jnp.zeros_like(hole_integrals[block_id]))
        hole_term = jnp.dot(weights.reshape(PB, NQ * PB), stacked, preferred_element_type=jnp.float32)
        return ladder + hole_term

    combined = lax.map(block_update, jnp.arange(NQ, dtype=jnp.int32))
    return jnp.where(valid[:, None, :], combined / denominators, jnp.float32(0.0)).astype(jnp.bfloat16)
```

```python
import functools

import jax
import jax.numpy as jnp
from jax import lax
from jax.experimental import pallas as pl
from jax.experimental.pallas import tpu as pltpu
from jax.sharding import PartitionSpec as P

MESH = pl.DeviceIdType.MESH
NQ, NIRR, BLK, KC, NA = 4, 8, 32, 1024, 1024
HALF = BLK // 2
MSG = NA + 128


def plane_of(b_y, b_x):
    return 2 * ((b_x + b_y) % 4) + b_y % 2, b_y // 2


def block_of(z, k):
    b_y = 2 * k + z % 2
    return b_y, (z // 2 + 4 - b_y) % 4


def encode(value):
    top = jnp.max(jnp.abs(value), axis=1, keepdims=True)
    step = jnp.ceil(8.0 * jnp.log2(jnp.maximum(top, 1e-30) * (1.0 / 32760.0)))
    scaled = jnp.round(value * jnp.exp2(step * -0.125))
    scaled = jnp.minimum(jnp.maximum(scaled, -32767.0), 32767.0)
    step = jnp.broadcast_to(step, (value.shape[0], 128))
    return scaled.astype(jnp.int32).astype(jnp.int16), step.astype(jnp.int32).astype(jnp.int16)


def widen(coded):
    low = coded.astype(jnp.int32) & 0xFFFF
    return ((low ^ 0x8000) - 0x8000).astype(jnp.float32)


def decode(coded, step):
    return widen(coded) * jnp.exp2(widen(step)[:, :1] * 0.125)


def kernel(pair_ref, used_ref, amp, ints, hole, den, out,
           tvm, g, wg, bt, dvm, am, wm, p_out, p_own, p_in, sbuf, rbuf,
           loc_sem, p1s, p1r, p2s, p2r, w0s, w0r, w1s, w1r, w2s, w2r, ats, atr, cs, cr, zs, zr):
    z, c, k = lax.axis_index("row"), lax.axis_index("col"), lax.axis_index("rep")
    y, x = c // 4, c % 4
    xh, xk = x // 2, x % 2
    r = 2 * z + k

    def xmate(d):
        return (z, y * 4 + (x + d) % 4, k)

    def ymate(d):
        return (z, ((y + d) % 4) * 4 + x, k)

    my_bz, my_bk = plane_of(y, x)
    own_y, own_x = block_of(z, k)
    phi_r = (r // 4 + r % 4) % 4
    phi_c = (c // 4 + c % 4) % 4
    w_to = (my_bz, r, my_bk)
    w_from = (c // 2, 4 * own_y + own_x, c % 2)
    xb = (x + phi_r) % 4
    yb = (y + phi_r) % 4
    z0, k0 = plane_of(y, xb)
    z1, k1 = plane_of(yb, x)
    a_to = ((z0, r, k0), (z1, r, k1))
    a_from = (
        (c // 2, 4 * own_y + (own_x + 4 - phi_c) % 4, c % 2),
        (c // 2, 4 * ((own_y + 4 - phi_c) % 4) + own_x, c % 2),
    )

    def is_me(dev):
        return (dev[0] == z) & (dev[1] == c) & (dev[2] == k)

    loads = [pltpu.make_async_copy(amp, g.at[:, y, xh, xk], loc_sem.at[0])]
    loads += [pltpu.make_async_copy(ints.at[q], tvm.at[q], loc_sem.at[1 + q]) for q in range(NQ)]
    loads += [pltpu.make_async_copy(den, dvm, loc_sem.at[5])]
    for load in loads:
        load.start()

    bar = pltpu.get_barrier_semaphore()

    def greet(dev):
        pl.semaphore_signal(bar, inc=1, device_id=dev, device_id_type=MESH)

    for d in (1, 2, 3):
        greet(xmate(d))
        greet(ymate(d))
    greet((z, c, 1 - k))
    greet(((z + 1) % 8, c, k))
    greet(((z + 7) % 8, c, k))
    for to, source in ((w_to, w_from), (a_to[0], a_from[0]), (a_to[1], a_from[1])):
        greet(to)
        greet(source)

    pl.semaphore_wait(bar, 15)

    def remote(src, dst, ssem, rsem, dev):
        return pltpu.make_async_remote_copy(
            src_ref=src, dst_ref=dst, send_sem=ssem, recv_sem=rsem, device_id=dev, device_id_type=MESH)

    def moved(src, dst, ssem, rsem, to):
        far = remote(src, dst, ssem, rsem, to)
        near = pltpu.make_async_copy(src, dst, rsem)

        def start():
            pl.when(is_me(to))(near.start)
            pl.when(jnp.logical_not(is_me(to)))(far.start)

        def wait():
            pl.when(is_me(to))(near.wait)
            pl.when(jnp.logical_not(is_me(to)))(far.wait)

        return start, wait

    lo, hi = pl.ds(0, HALF), pl.ds(HALF, HALF)
    w_start, w_wait = moved(hole, wg.at[:, r // 4, (r % 4) // 2, r % 2], w0s, w0r, w_to)
    w_start()

    def first(q):
        cps = []
        for d in (1, 2, 3):
            cps.append(remote(amp.at[q, lo], g.at[q, y, xh, xk, lo], p1s.at[q, 0, d - 1], p1r.at[q, 0, d - 1], xmate(d)))
            cps.append(remote(amp.at[q, hi], g.at[q, y, xh, xk, hi], p1s.at[q, 1, d - 1], p1r.at[q, 1, d - 1], ymate(d)))
        return cps

    def second(q):
        cps = []
        for d in (1, 2, 3):
            row = g.at[q, y, :, :, lo]
            col = g.at[q, :, xh, xk, hi]
            cps.append(remote(row, row, p2s.at[q, 0, d - 1], p2r.at[q, 0, d - 1], ymate(d)))
            cps.append(remote(col, col, p2s.at[q, 1, d - 1], p2r.at[q, 1, d - 1], xmate(d)))
        return cps

    firsts = [first(q) for q in range(NQ)]
    seconds = [second(q) for q in range(NQ)]
    w_first, w_second = [], []
    for d in (1, 2, 3):
        own_lo, own_hi = wg.at[:, y, xh, xk, lo], wg.at[:, y, xh, xk, hi]
        row, col = wg.at[:, y, :, :, lo], wg.at[:, :, xh, xk, hi]
        w_first.append(remote(own_lo, own_lo, w1s.at[0, d - 1], w1r.at[0, d - 1], xmate(d)))
        w_first.append(remote(own_hi, own_hi, w1s.at[1, d - 1], w1r.at[1, d - 1], ymate(d)))
        w_second.append(remote(row, row, w2s.at[0, d - 1], w2r.at[0, d - 1], ymate(d)))
        w_second.append(remote(col, col, w2s.at[1, d - 1], w2r.at[1, d - 1], xmate(d)))

    for q in range(NQ):
        for cp in firsts[q]:
            cp.start()
    loads[0].wait()

    def finish_first(q):
        for cp in firsts[q]:
            cp.wait()
        for cp in seconds[q]:
            cp.start()

    finish_first(0)
    w_wait()
    for cp in w_first:
        cp.start()
    for q in range(1, NQ):
        finish_first(q)

    at0 = moved(g.at[:, y, xb // 2, xb % 2, lo], bt.at[:, lo], ats.at[0], atr.at[0], a_to[0])
    at1 = moved(g.at[:, yb, xh, xk, hi], bt.at[:, hi], ats.at[1], atr.at[1], a_to[1])
    at0[0]()
    at1[0]()
    for cp in w_first:
        cp.wait()
    for cp in w_second:
        cp.start()

    limits = []
    for q in range(NQ):
        limit = 0
        for i in range(NIRR):
            limit = limit + jnp.where(pair_ref[q] == i, used_ref[i], 0)
        limits.append(limit)
    lane = lax.broadcasted_iota(jnp.int32, (HALF, KC), 1)
    lane_w = lax.broadcasted_iota(jnp.int32, (HALF, 128), 1) // BLK
    out_lane = lax.broadcasted_iota(jnp.int32, (BLK, NA), 1)

    def keep(rows, mask):
        tiles = rows.reshape(-1, HALF, rows.shape[-1]) * mask[None]
        return tiles.reshape(rows.shape)

    for cp in w_second:
        cp.wait()
    at0[1]()
    at1[1]()
    for q in range(NQ):
        inside = jnp.where(c * NA + lane < limits[q], 1.0, 0.0).astype(jnp.bfloat16)
        bt[q] = keep(bt[q], inside)

    def product(q, side, dst):
        inside = jnp.where(r * KC + lane < limits[q], 1.0, 0.0).astype(jnp.bfloat16)
        am[...] = keep(g[q, :, :, side].reshape(8 * BLK, KC), inside)
        alike = jnp.zeros((HALF, 128), jnp.float32)
        for q2 in range(NQ):
            same = jnp.where(pair_ref[q] == pair_ref[q2], 1.0, 0.0)
            alike = jnp.where(lane_w == q2, same, alike)
        wm[...] = keep(wg[q, :, :, side].reshape(8 * BLK, 128), alike.astype(jnp.bfloat16))

        @pl.loop(0, NA // 256)
        def _(n):
            cols = pl.ds(pl.multiple_of(n * 256, 256), 256)
            total = jnp.dot(am[...], tvm[q, :, cols], preferred_element_type=jnp.float32)
            held = bt[:, :, cols].reshape(NQ * BLK, 256)
            total += jnp.dot(wm[...], held, preferred_element_type=jnp.float32)
            dst[q, :, :, cols] = total.reshape(8, BLK, 256)

    swaps = [remote(p_out.at[q], p_in.at[q], cs.at[q], cr.at[q], (z, c, 1 - k)) for q in range(NQ)]

    def compute(q):
        loads[1 + q].wait()
        for cp in seconds[q]:
            cp.wait()
        product(q, 1 - k, p_out)
        swaps[q].start()
        product(q, k, p_own)

    def hops(q, way):
        return 4 if (q + way) % 2 == 0 else 3

    def link(q, way, h):
        i = way * 4 + h
        to = (z + 1) % 8 if way == 0 else (z + 7) % 8
        return remote(sbuf.at[q, i], rbuf.at[q, i], zs.at[q, i], zr.at[q, i], (to, c, k))

    def received(q, way, h):
        i = way * 4 + h
        link(q, way, h).wait_recv()
        return decode(rbuf[q, i, :, :NA], rbuf[q, i, :, NA:])

    def hop(q, h):
        for way in (0, 1):
            n = hops(q, way)
            if h >= n:
                continue
            far = n - h
            owner = (z + far) % 8 if way == 0 else (z + 8 - far) % 8
            total = p_own[q, owner] + p_in[q, owner]
            if h > 0:
                total += received(q, way, h - 1)
            coded, step = encode(total)
            i = way * 4 + h
            sbuf[q, i, :, :NA] = coded
            sbuf[q, i, :, NA:] = step
            link(q, way, h).start()

    def final(q):
        total = p_own[q, z] + p_in[q, z]
        total += received(q, 0, hops(q, 0) - 1)
        total += received(q, 1, hops(q, 1) - 1)
        total = total / dvm[q]
        out[q] = jnp.where(c * NA + out_lane < limits[q], total, 0.0).astype(jnp.bfloat16)

    for s in range(NQ + 5):
        t = s - 1
        if 0 <= t < NQ:
            swaps[t].wait()
            hop(t, 0)
        if s == 1:
            loads[5].wait()
        for h in (1, 2, 3):
            t = s - 1 - h
            if 0 <= t < NQ:
                hop(t, h)
        t = s - 5
        if 0 <= t < NQ:
            final(t)
        if s < NQ:
            compute(s)

    for q in range(NQ):
        for way in (0, 1):
            for h in range(hops(q, way)):
                link(q, way, h).wait_send()


def per_device(amplitudes, ladder_integrals, hole_integrals, denominators, pair_irrep, irrep_pairs):
    hole = hole_integrals.reshape(NQ, BLK, NQ * BLK)
    anywhere = pl.BlockSpec(memory_space=pl.ANY)
    smem = pl.BlockSpec(memory_space=pltpu.SMEM)
    bf16, f32 = jnp.bfloat16, jnp.float32
    dma = pltpu.SemaphoreType.DMA
    return pl.pallas_call(
        kernel,
        out_shape=jax.ShapeDtypeStruct((NQ, BLK, NA), bf16),
        in_specs=[smem, smem, anywhere, anywhere, anywhere, anywhere],
        out_specs=pl.BlockSpec(memory_space=pltpu.VMEM),
        scratch_shapes=[
            pltpu.VMEM((NQ, KC, NA), bf16),
            pltpu.VMEM((NQ, 4, 2, 2, BLK, KC), bf16),
            pltpu.VMEM((NQ, 4, 2, 2, BLK, 128), bf16),
            pltpu.VMEM((NQ, BLK, NA), bf16),
            pltpu.VMEM((NQ, BLK, NA), f32),
            pltpu.VMEM((8 * BLK, KC), bf16),
            pltpu.VMEM((8 * BLK, 128), bf16),
            pltpu.VMEM((NQ, 8, BLK, NA), f32),
            pltpu.VMEM((NQ, 8, BLK, NA), f32),
            pltpu.VMEM((NQ, 8, BLK, NA), f32),
            pltpu.VMEM((NQ, 8, BLK, MSG), jnp.int16),
            pltpu.VMEM((NQ, 8, BLK, MSG), jnp.int16),
            dma((6,)),
            dma((NQ, 2, 3)), dma((NQ, 2, 3)), dma((NQ, 2, 3)), dma((NQ, 2, 3)),
            dma, dma,
            dma((2, 3)), dma((2, 3)), dma((2, 3)), dma((2, 3)),
            dma((2,)), dma((2,)),
            dma((NQ,)), dma((NQ,)),
            dma((NQ, 8)), dma((NQ, 8)),
        ],
        compiler_params=pltpu.CompilerParams(
            collective_id=0, has_side_effects=True, vmem_limit_bytes=52 * 1024 * 1024),
    )(pair_irrep, irrep_pairs, amplitudes, ladder_integrals, hole, denominators)


def solution(mesh):
    return jax.shard_map(
        per_device,
        mesh=mesh,
        in_specs=(
            P(None, "col", ("row", "rep")),
            P(None, ("row", "rep"), "col"),
            P(None, ("row", "rep"), None, "col"),
            P(None, ("row", "rep"), "col"),
            P(),
            P(),
        ),
        out_specs=P(None, ("row", "rep"), "col"),
        check_vma=False,
    )
```

```python
import functools

import jax
import jax.numpy as jnp
from jax import lax
from jax.experimental import pallas as pl
from jax.experimental.pallas import tpu as pltpu
from jax.sharding import PartitionSpec as P

MESH = pl.DeviceIdType.MESH
NQ, NIRR, BLK, KC, NA = 4, 8, 32, 1024, 1024
HALF = BLK // 2
MSG = NA + 128
CHUNKS = [(q, pl.ds(0, BLK)) for q in range(NQ - 1)] + [(NQ - 1, pl.ds(0, HALF)), (NQ - 1, pl.ds(HALF, HALF))]
NT = len(CHUNKS)
CHAINED = 2
WIDE = 512


def plane_of(b_y, b_x):
    return 2 * ((b_x + b_y) % 4) + b_y % 2, b_y // 2


def block_of(z, k):
    b_y = 2 * k + z % 2
    return b_y, (z // 2 + 4 - b_y) % 4


def encode(value):
    top = jnp.max(jnp.abs(value), axis=1, keepdims=True)
    step = jnp.ceil(8.0 * jnp.log2(jnp.maximum(top, 1e-30) * (1.0 / 32760.0)))
    scaled = jnp.round(value * jnp.exp2(step * -0.125))
    scaled = jnp.minimum(jnp.maximum(scaled, -32767.0), 32767.0)
    step = jnp.broadcast_to(step, (value.shape[0], 128))
    return scaled.astype(jnp.int32).astype(jnp.int16), step.astype(jnp.int32).astype(jnp.int16)


def widen(coded):
    low = coded.astype(jnp.int32) & 0xFFFF
    return ((low ^ 0x8000) - 0x8000).astype(jnp.float32)


def decode(coded, step):
    return widen(coded) * jnp.exp2(widen(step)[:, :1] * 0.125)


def kernel(pair_ref, used_ref, amp, ints, hole, den, out,
           tvm, g, wg, bt, dvm, am, wm, p_out, p_own, p_in, sbuf, rbuf,
           loc_sem, p1s, p1r, p2s, p2r, p3s, p3r, w0s, w0r, w1s, w1r, w2s, w2r, as_, ar, cs, cr, zs, zr):
    z, c, k = lax.axis_index("row"), lax.axis_index("col"), lax.axis_index("rep")
    y, x = c // 4, c % 4
    xh, xk = x // 2, x % 2
    r = 2 * z + k

    def xmate(d):
        return (z, y * 4 + (x + d) % 4, k)

    def ymate(d):
        return (z, ((y + d) % 4) * 4 + x, k)

    my_bz, my_bk = plane_of(y, x)
    own_y, own_x = block_of(z, k)
    phi_r = (r // 4 + r % 4) % 4
    phi_c = (c // 4 + c % 4) % 4
    w_to = (my_bz, r, my_bk)
    w_from = (c // 2, 4 * own_y + own_x, c % 2)
    xb = (x + phi_r) % 4
    yb = (y + phi_r) % 4
    z0, k0 = plane_of(y, xb)
    z1, k1 = plane_of(yb, x)
    a_to = ((z0, r, k0), (z1, r, k1))
    a_from = (
        (c // 2, 4 * own_y + (own_x + 4 - phi_c) % 4, c % 2),
        (c // 2, 4 * ((own_y + 4 - phi_c) % 4) + own_x, c % 2),
    )

    def is_me(dev):
        return (dev[0] == z) & (dev[1] == c) & (dev[2] == k)

    loads = [pltpu.make_async_copy(amp, g.at[:, y, xh, xk], loc_sem.at[0])]
    loads += [pltpu.make_async_copy(ints.at[q], tvm.at[q], loc_sem.at[1 + q]) for q in range(NQ)]
    loads += [pltpu.make_async_copy(den, dvm, loc_sem.at[5])]
    for load in loads:
        load.start()

    bar = pltpu.get_barrier_semaphore()

    def greet(dev):
        pl.semaphore_signal(bar, inc=1, device_id=dev, device_id_type=MESH)

    for d in (1, 2, 3):
        greet(xmate(d))
        greet(ymate(d))
    greet((z, c, 1 - k))
    for d in (1, 2, 6, 7):
        greet(((z + d) % 8, c, k))
    for to, source in ((w_to, w_from), (a_to[0], a_from[0]), (a_to[1], a_from[1])):
        greet(to)
        greet(source)

    pl.semaphore_wait(bar, 17)

    def remote(src, dst, ssem, rsem, dev):
        return pltpu.make_async_remote_copy(
            src_ref=src, dst_ref=dst, send_sem=ssem, recv_sem=rsem, device_id=dev, device_id_type=MESH)

    def moved(src, dst, ssem, rsem, to):
        far = remote(src, dst, ssem, rsem, to)
        near = pltpu.make_async_copy(src, dst, rsem)

        def start():
            pl.when(is_me(to))(near.start)
            pl.when(jnp.logical_not(is_me(to)))(far.start)

        def wait():
            pl.when(is_me(to))(near.wait)
            pl.when(jnp.logical_not(is_me(to)))(far.wait)

        return start, wait

    lo, hi = pl.ds(0, HALF), pl.ds(HALF, HALF)
    w_start, w_wait = moved(hole, wg.at[:, r // 4, (r % 4) // 2, r % 2], w0s, w0r, w_to)
    w_start()

    left, right = pl.ds(0, KC // 2), pl.ds(KC // 2, KC // 2)
    y_up, y_dn, x_up, x_dn = (y + 1) % 4, (y + 3) % 4, (x + 1) % 4, (x + 3) % 4

    def first(q):
        cps = []
        for d in (1, 2, 3):
            cps.append(remote(amp.at[q, :, left], g.at[q, y, xh, xk, :, left], p1s.at[q, 0, d - 1], p1r.at[q, 0, d - 1], xmate(d)))
            cps.append(remote(amp.at[q, :, right], g.at[q, y, xh, xk, :, right], p1s.at[q, 1, d - 1], p1r.at[q, 1, d - 1], ymate(d)))
        return cps

    def second(t):
        q, rows = CHUNKS[t]
        row = g.at[q, y, :, :, rows, left]
        col = g.at[q, :, xh, xk, rows, right]
        cps = []
        for i, d in enumerate((1, 3)):
            cps.append(remote(row, row, p2s.at[t, 0, i], p2r.at[t, 0, i], ymate(d)))
            cps.append(remote(col, col, p2s.at[t, 1, i], p2r.at[t, 1, i], xmate(d)))
        return cps

    def third(t):
        q, rows = CHUNKS[t]
        pieces = (
            (g.at[q, y_dn, 0, :, rows, left], ymate(1)),
            (g.at[q, y_up, 1, :, rows, left], ymate(3)),
            (g.at[q, pl.ds(0, 2), x_dn // 2, x_dn % 2, rows, right], xmate(1)),
            (g.at[q, pl.ds(2, 2), x_up // 2, x_up % 2, rows, right], xmate(3)),
        )
        return [remote(ref, ref, p3s.at[t, i], p3r.at[t, i], to) for i, (ref, to) in enumerate(pieces)]

    firsts = [first(q) for q in range(NQ)]
    seconds = [second(t) for t in range(NT)]
    thirds = [third(t) for t in range(NT)]
    w_first, w_second = [], []
    for d in (1, 2, 3):
        own_lo, own_hi = wg.at[:, y, xh, xk, lo], wg.at[:, y, xh, xk, hi]
        row, col = wg.at[:, y, :, :, lo], wg.at[:, :, xh, xk, hi]
        w_first.append(remote(own_lo, own_lo, w1s.at[0, d - 1], w1r.at[0, d - 1], xmate(d)))
        w_first.append(remote(own_hi, own_hi, w1s.at[1, d - 1], w1r.at[1, d - 1], ymate(d)))
        w_second.append(remote(row, row, w2s.at[0, d - 1], w2r.at[0, d - 1], ymate(d)))
        w_second.append(remote(col, col, w2s.at[1, d - 1], w2r.at[1, d - 1], xmate(d)))

    def start(cps):
        for cp in cps:
            cp.start()

    def wait(cps):
        for cp in cps:
            cp.wait()

    ats = [
        (
            moved(g.at[q, y, xb // 2, xb % 2, :, left], bt.at[q, :, left], as_.at[q, 0], ar.at[q, 0], a_to[0]),
            moved(g.at[q, yb, xh, xk, :, right], bt.at[q, :, right], as_.at[q, 1], ar.at[q, 1], a_to[1]),
        )
        for q in range(NQ)
    ]

    def at_start(q):
        for go, _ in ats[q]:
            go()

    def at_wait(q):
        for _, hold in ats[q]:
            hold()

    for q in range(NQ):
        start(firsts[q])
    loads[0].wait()

    limits = []
    for q in range(NQ):
        limit = 0
        for i in range(NIRR):
            limit = limit + jnp.where(pair_ref[q] == i, used_ref[i], 0)
        limits.append(limit)
    lane = lax.broadcasted_iota(jnp.int32, (HALF, KC), 1)
    lane_w = lax.broadcasted_iota(jnp.int32, (HALF, 128), 1) // BLK

    def keep(rows, mask):
        tiles = rows.reshape(-1, HALF, rows.shape[-1]) * mask[None]
        return tiles.reshape(rows.shape)

    def mask_bt(q):
        inside = jnp.where(c * NA + lane < limits[q], 1.0, 0.0).astype(jnp.bfloat16)
        bt[q] = keep(bt[q], inside)

    def ladder(t, side, dst):
        q, rows = CHUNKS[t]
        m = 8 * rows.size
        inside = jnp.where(r * KC + lane < limits[q], 1.0, 0.0).astype(jnp.bfloat16)
        am[:m] = keep(g[q, :, :, side, rows].reshape(m, KC), inside)

        @pl.loop(0, NA // WIDE)
        def _(n):
            cols = pl.ds(pl.multiple_of(n * WIDE, WIDE), WIDE)
            total = jnp.dot(am[:m], tvm[q, :, cols], preferred_element_type=jnp.float32)
            dst[q, :, rows, cols] = total.reshape(8, rows.size, WIDE)

    def add_hole(t, side, dst):
        q, rows = CHUNKS[t]
        m = 8 * rows.size
        alike = jnp.zeros((HALF, 128), jnp.float32)
        for q2 in range(NQ):
            same = jnp.where(pair_ref[q] == pair_ref[q2], 1.0, 0.0)
            alike = jnp.where(lane_w == q2, same, alike)
        wm[:m] = keep(wg[q, :, :, side, rows].reshape(m, 128), alike.astype(jnp.bfloat16))

        @pl.loop(0, NA // WIDE)
        def _(n):
            cols = pl.ds(pl.multiple_of(n * WIDE, WIDE), WIDE)
            held = bt[:, :, cols].reshape(NQ * BLK, WIDE)
            total = jnp.dot(wm[:m], held, preferred_element_type=jnp.float32)
            dst[q, :, rows, cols] += total.reshape(8, rows.size, WIDE)

    swaps = []
    for t, (q, rows) in enumerate(CHUNKS):
        swaps.append(remote(p_out.at[q, :, rows], p_in.at[q, :, rows], cs.at[t], cr.at[t], (z, c, 1 - k)))

    def outer(t):
        ladder(t, 1 - k, p_out)
        add_hole(t, 1 - k, p_out)
        swaps[t].start()

    def inner(t):
        ladder(t, k, p_own)
        add_hole(t, k, p_own)

    def partial(t, owner):
        q, rows = CHUNKS[t]
        return p_own[q, owner, rows] + p_in[q, owner, rows]

    def post(t, i, total):
        n = CHUNKS[t][1].size
        coded, step = encode(total)
        sbuf[t, i, :n, :NA] = coded
        sbuf[t, i, :n, NA:] = step

    def letter(t, i, to):
        n = CHUNKS[t][1].size
        return remote(sbuf.at[t, i, :n], rbuf.at[t, i, :n], zs.at[t, i], zr.at[t, i], (to, c, k))

    def read(t, i):
        n = CHUNKS[t][1].size
        letter(t, i, (z + 1) % 8).wait_recv()
        return decode(rbuf[t, i, :n, :NA], rbuf[t, i, :n, NA:])

    def send_along(t, i, d, total):
        post(t, i, total)
        letter(t, i, (z + d + 8) % 8).start()

    def mine(t, d):
        return partial(t, (z + d + 8) % 8)

    def hops(t, way):
        return 4 if (t + way) % 2 == 0 else 3

    def chain(t, h):
        for way, d in ((0, 1), (1, -1)):
            n = hops(t, way)
            if h < n:
                total = mine(t, d * (n - h))
                if h > 0:
                    total += read(t, way * 4 + h - 1)
                send_along(t, way * 4 + h, d, total)

    def first_round(t):
        send_along(t, 4, -2 if t % 2 == 0 else 2, mine(t, 4))
        send_along(t, 1, 1, mine(t, 3))
        send_along(t, 2, -1, mine(t, -3))
        send_along(t, 0, 1, mine(t, -1))
        send_along(t, 3, -1, mine(t, 1))

    def second_round(t):
        down = mine(t, -2) + read(t, 0) + read(t, 2)
        up = mine(t, 2) + read(t, 1) + read(t, 3)
        if t % 2 == 0:
            send_along(t, 6, 2, up)
            send_along(t, 5, -2, down + read(t, 4))
        else:
            send_along(t, 5, -2, down)
            send_along(t, 6, 2, up + read(t, 4))

    def final(t):
        q, rows = CHUNKS[t]
        if t < CHAINED:
            total = mine(t, 0) + read(t, hops(t, 0) - 1) + read(t, 4 + hops(t, 1) - 1)
        else:
            total = mine(t, 0) + read(t, 5) + read(t, 6)
        total = total / dvm[q, rows]
        lanes = lax.broadcasted_iota(jnp.int32, (rows.size, NA), 1)
        out[q, rows] = jnp.where(c * NA + lanes < limits[q], total, 0.0).astype(jnp.bfloat16)

    def reduce(t):
        swaps[t].wait()
        if t < CHAINED:
            chain(t, 0)
        else:
            first_round(t)

    wait(firsts[0])
    start(seconds[0])
    at_start(0)
    for q in range(1, NQ):
        wait(firsts[q])
        at_start(q)
    w_wait()
    start(w_first)
    start(seconds[1])
    wait(seconds[0])
    start(thirds[0])
    wait(w_first)
    start(w_second)
    start(seconds[2])
    wait(seconds[1])
    start(thirds[1])
    start(seconds[3])
    start(seconds[4])
    for load in loads[1:]:
        load.wait()
    wait(thirds[0])
    ladder(0, 1 - k, p_out)
    ladder(0, k, p_own)
    wait(w_second)
    for q in range(NQ):
        at_wait(q)
        mask_bt(q)
    add_hole(0, 1 - k, p_out)
    swaps[0].start()
    add_hole(0, k, p_own)
    wait(seconds[2])
    start(thirds[2])
    wait(thirds[1])
    outer(1)
    reduce(0)
    inner(1)
    wait(seconds[3])
    start(thirds[3])
    wait(seconds[4])
    start(thirds[4])
    reduce(1)
    wait(thirds[2])
    outer(2)
    chain(0, 1)
    inner(2)
    wait(thirds[3])
    outer(3)
    reduce(2)
    chain(1, 1)
    inner(3)
    wait(thirds[4])
    outer(4)
    chain(0, 2)
    reduce(3)
    inner(4)
    reduce(4)
    chain(1, 2)
    second_round(2)
    chain(0, 3)
    second_round(3)
    chain(1, 3)
    second_round(4)
    final(0)
    final(2)
    final(3)
    final(1)
    final(4)

    for t in range(NT):
        used = range(7) if t >= CHAINED else [w * 4 + h for w in (0, 1) for h in range(hops(t, w))]
        for i in used:
            letter(t, i, (z + 1) % 8).wait_send()


def per_device(amplitudes, ladder_integrals, hole_integrals, denominators, pair_irrep, irrep_pairs):
    hole = hole_integrals.reshape(NQ, BLK, NQ * BLK)
    anywhere = pl.BlockSpec(memory_space=pl.ANY)
    smem = pl.BlockSpec(memory_space=pltpu.SMEM)
    bf16, f32 = jnp.bfloat16, jnp.float32
    dma = pltpu.SemaphoreType.DMA
    return pl.pallas_call(
        kernel,
        out_shape=jax.ShapeDtypeStruct((NQ, BLK, NA), bf16),
        in_specs=[smem, smem, anywhere, anywhere, anywhere, anywhere],
        out_specs=pl.BlockSpec(memory_space=pltpu.VMEM),
        scratch_shapes=[
            pltpu.VMEM((NQ, KC, NA), bf16),
            pltpu.VMEM((NQ, 4, 2, 2, BLK, KC), bf16),
            pltpu.VMEM((NQ, 4, 2, 2, BLK, 128), bf16),
            pltpu.VMEM((NQ, BLK, NA), bf16),
            pltpu.VMEM((NQ, BLK, NA), f32),
            pltpu.VMEM((8 * BLK, KC), bf16),
            pltpu.VMEM((8 * BLK, 128), bf16),
            pltpu.VMEM((NQ, 8, BLK, NA), f32),
            pltpu.VMEM((NQ, 8, BLK, NA), f32),
            pltpu.VMEM((NQ, 8, BLK, NA), f32),
            pltpu.VMEM((NT, 8, BLK, MSG), jnp.int16),
            pltpu.VMEM((NT, 8, BLK, MSG), jnp.int16),
            dma((6,)),
            dma((NQ, 2, 3)), dma((NQ, 2, 3)), dma((NT, 2, 2)), dma((NT, 2, 2)), dma((NT, 4)), dma((NT, 4)),
            dma, dma,
            dma((2, 3)), dma((2, 3)), dma((2, 3)), dma((2, 3)),
            dma((NQ, 2)), dma((NQ, 2)),
            dma((NT,)), dma((NT,)),
            dma((NT, 8)), dma((NT, 8)),
        ],
        compiler_params=pltpu.CompilerParams(
            collective_id=0, has_side_effects=True, vmem_limit_bytes=60 * 1024 * 1024),
    )(pair_irrep, irrep_pairs, amplitudes, ladder_integrals, hole, denominators)


def solution(mesh):
    return jax.shard_map(
        per_device,
        mesh=mesh,
        in_specs=(
            P(None, "col", ("row", "rep")),
            P(None, ("row", "rep"), "col"),
            P(None, ("row", "rep"), None, "col"),
            P(None, ("row", "rep"), "col"),
            P(),
            P(),
        ),
        out_specs=P(None, ("row", "rep"), "col"),
        check_vma=False,
    )
```

```python
import functools

import jax
import jax.numpy as jnp
from jax import lax
from jax.experimental import pallas as pl
from jax.experimental.pallas import tpu as pltpu
from jax.sharding import PartitionSpec as P

MESH = pl.DeviceIdType.MESH
NQ, NIRR, BLK, KC, NA = 4, 8, 32, 1024, 1024
HALF = BLK // 2
MSG = NA + 128
CHUNKS = [(q, pl.ds(0, BLK)) for q in range(NQ - 1)] + [(NQ - 1, pl.ds(0, HALF)), (NQ - 1, pl.ds(HALF, HALF))]
NT = len(CHUNKS)
CHAINED = 3
WIDE = 1024


def plane_of(b_y, b_x):
    return 2 * ((b_x + b_y) % 4) + b_y % 2, b_y // 2


def block_of(z, k):
    b_y = 2 * k + z % 2
    return b_y, (z // 2 + 4 - b_y) % 4


def encode(value):
    top = jnp.max(jnp.abs(value), axis=1, keepdims=True)
    step = jnp.ceil(8.0 * jnp.log2(jnp.maximum(top, 1e-30) * (1.0 / 32760.0)))
    scaled = jnp.round(value * jnp.exp2(step * -0.125))
    scaled = jnp.minimum(jnp.maximum(scaled, -32767.0), 32767.0)
    step = jnp.broadcast_to(step, (value.shape[0], 128))
    return scaled.astype(jnp.int32).astype(jnp.int16), step.astype(jnp.int32).astype(jnp.int16)


def widen(coded):
    low = coded.astype(jnp.int32) & 0xFFFF
    return ((low ^ 0x8000) - 0x8000).astype(jnp.float32)


def decode(coded, step):
    return widen(coded) * jnp.exp2(widen(step)[:, :1] * 0.125)


def kernel(pair_ref, used_ref, amp, ints, hole, den, out,
           tvm, g, wg, bt, dvm, am, wm, p_out, p_own, p_in, sbuf, rbuf,
           loc_sem, p1s, p1r, p2s, p2r, p3s, p3r, w0s, w0r, w1s, w1r, w2s, w2r, as_, ar, cs, cr, zs, zr):
    z, c, k = lax.axis_index("row"), lax.axis_index("col"), lax.axis_index("rep")
    y, x = c // 4, c % 4
    xh, xk = x // 2, x % 2
    r = 2 * z + k

    def xmate(d):
        return (z, y * 4 + (x + d) % 4, k)

    def ymate(d):
        return (z, ((y + d) % 4) * 4 + x, k)

    my_bz, my_bk = plane_of(y, x)
    own_y, own_x = block_of(z, k)
    phi_r = (r // 4 + r % 4) % 4
    phi_c = (c // 4 + c % 4) % 4
    w_to = (my_bz, r, my_bk)
    w_from = (c // 2, 4 * own_y + own_x, c % 2)
    xb = (x + phi_r) % 4
    yb = (y + phi_r) % 4
    z0, k0 = plane_of(y, xb)
    z1, k1 = plane_of(yb, x)
    a_to = ((z0, r, k0), (z1, r, k1))
    a_from = (
        (c // 2, 4 * own_y + (own_x + 4 - phi_c) % 4, c % 2),
        (c // 2, 4 * ((own_y + 4 - phi_c) % 4) + own_x, c % 2),
    )

    def is_me(dev):
        return (dev[0] == z) & (dev[1] == c) & (dev[2] == k)

    loads = [pltpu.make_async_copy(amp, g.at[:, y, xh, xk], loc_sem.at[0])]
    loads += [pltpu.make_async_copy(ints.at[q], tvm.at[q], loc_sem.at[1 + q]) for q in range(NQ)]
    loads += [pltpu.make_async_copy(den, dvm, loc_sem.at[5])]
    for load in loads:
        load.start()

    bar = pltpu.get_barrier_semaphore()

    def greet(dev):
        pl.semaphore_signal(bar, inc=1, device_id=dev, device_id_type=MESH)

    for d in (1, 2, 3):
        greet(xmate(d))
        greet(ymate(d))
    greet((z, c, 1 - k))
    for d in (1, 2, 6, 7):
        greet(((z + d) % 8, c, k))
    for to, source in ((w_to, w_from), (a_to[0], a_from[0]), (a_to[1], a_from[1])):
        greet(to)
        greet(source)

    pl.semaphore_wait(bar, 17)

    def remote(src, dst, ssem, rsem, dev):
        return pltpu.make_async_remote_copy(
            src_ref=src, dst_ref=dst, send_sem=ssem, recv_sem=rsem, device_id=dev, device_id_type=MESH)

    def moved(src, dst, ssem, rsem, to):
        far = remote(src, dst, ssem, rsem, to)
        near = pltpu.make_async_copy(src, dst, rsem)

        def start():
            pl.when(is_me(to))(near.start)
            pl.when(jnp.logical_not(is_me(to)))(far.start)

        def wait():
            pl.when(is_me(to))(near.wait)
            pl.when(jnp.logical_not(is_me(to)))(far.wait)

        return start, wait

    w_start, w_wait = moved(hole, wg.at[r // 4, (r % 4) // 2, r % 2], w0s, w0r, w_to)
    w_start()

    left, right = pl.ds(0, KC // 2), pl.ds(KC // 2, KC // 2)
    y_up, y_dn, x_up, x_dn = (y + 1) % 4, (y + 3) % 4, (x + 1) % 4, (x + 3) % 4

    def first(q):
        cps = []
        for d in (1, 2, 3):
            cps.append(remote(amp.at[q, :, left], g.at[q, y, xh, xk, :, left], p1s.at[q, 0, d - 1], p1r.at[q, 0, d - 1], xmate(d)))
            cps.append(remote(amp.at[q, :, right], g.at[q, y, xh, xk, :, right], p1s.at[q, 1, d - 1], p1r.at[q, 1, d - 1], ymate(d)))
        return cps

    def second(t):
        q, rows = CHUNKS[t]
        row = g.at[q, y, :, :, rows, left]
        col = g.at[q, :, xh, xk, rows, right]
        cps = []
        for i, d in enumerate((1, 3)):
            cps.append(remote(row, row, p2s.at[t, 0, i], p2r.at[t, 0, i], ymate(d)))
            cps.append(remote(col, col, p2s.at[t, 1, i], p2r.at[t, 1, i], xmate(d)))
        return cps

    def third(t):
        q, rows = CHUNKS[t]
        pieces = (
            (g.at[q, y_dn, 0, :, rows, left], ymate(1)),
            (g.at[q, y_up, 1, :, rows, left], ymate(3)),
            (g.at[q, pl.ds(0, 2), x_dn // 2, x_dn % 2, rows, right], xmate(1)),
            (g.at[q, pl.ds(2, 2), x_up // 2, x_up % 2, rows, right], xmate(3)),
        )
        return [remote(ref, ref, p3s.at[t, i], p3r.at[t, i], to) for i, (ref, to) in enumerate(pieces)]

    firsts = [first(q) for q in range(NQ)]
    seconds = [second(t) for t in range(NT)]
    thirds = [third(t) for t in range(NT)]
    w_first, w_second = [], []
    for d in (1, 2, 3):
        own_lo, own_hi = wg.at[y, xh, xk, :2], wg.at[y, xh, xk, 2:]
        row, col = wg.at[y, :, :, :2], wg.at[:, xh, xk, 2:]
        w_first.append(remote(own_lo, own_lo, w1s.at[0, d - 1], w1r.at[0, d - 1], xmate(d)))
        w_first.append(remote(own_hi, own_hi, w1s.at[1, d - 1], w1r.at[1, d - 1], ymate(d)))
        w_second.append(remote(row, row, w2s.at[0, d - 1], w2r.at[0, d - 1], ymate(d)))
        w_second.append(remote(col, col, w2s.at[1, d - 1], w2r.at[1, d - 1], xmate(d)))

    def start(cps):
        for cp in cps:
            cp.start()

    def wait(cps):
        for cp in cps:
            cp.wait()

    ats = [
        (
            moved(g.at[q, y, xb // 2, xb % 2, :, left], bt.at[q, :, left], as_.at[q, 0], ar.at[q, 0], a_to[0]),
            moved(g.at[q, yb, xh, xk, :, right], bt.at[q, :, right], as_.at[q, 1], ar.at[q, 1], a_to[1]),
        )
        for q in range(NQ)
    ]

    def at_start(q):
        for go, _ in ats[q]:
            go()

    def at_wait(q):
        for _, hold in ats[q]:
            hold()

    for q in range(NQ):
        start(firsts[q])
    loads[0].wait()

    limits = []
    for q in range(NQ):
        limit = 0
        for i in range(NIRR):
            limit = limit + jnp.where(pair_ref[q] == i, used_ref[i], 0)
        limits.append(limit)
    lane = lax.broadcasted_iota(jnp.int32, (HALF, KC), 1)
    lane_w = lax.broadcasted_iota(jnp.int32, (HALF, 128), 1) // BLK

    def keep(rows, mask):
        tiles = rows.reshape(-1, HALF, rows.shape[-1]) * mask[None]
        return tiles.reshape(rows.shape)

    def mask_bt(q):
        inside = jnp.where(c * NA + lane < limits[q], 1.0, 0.0).astype(jnp.bfloat16)
        bt[q] = keep(bt[q], inside)

    def ladder(t, side, dst):
        q, rows = CHUNKS[t]
        m = 8 * rows.size
        inside = jnp.where(r * KC + lane < limits[q], 1.0, 0.0).astype(jnp.bfloat16)
        am[:m] = keep(g[q, :, :, side, rows].reshape(m, KC), inside)

        @pl.loop(0, NA // WIDE)
        def _(n):
            cols = pl.ds(pl.multiple_of(n * WIDE, WIDE), WIDE)
            total = jnp.dot(am[:m], tvm[q, :, cols], preferred_element_type=jnp.float32)
            dst[q, :, rows, cols] = total.reshape(8, rows.size, WIDE)

    def add_hole(t, side, dst):
        q, rows = CHUNKS[t]
        m = 8 * rows.size
        alike = jnp.zeros((HALF, 128), jnp.float32)
        for q2 in range(NQ):
            same = jnp.where(pair_ref[q] == pair_ref[q2], 1.0, 0.0)
            alike = jnp.where(lane_w == q2, same, alike)
        wm[:m] = keep(wg[:, :, side, q, rows].reshape(m, 128), alike.astype(jnp.bfloat16))

        @pl.loop(0, NA // WIDE)
        def _(n):
            cols = pl.ds(pl.multiple_of(n * WIDE, WIDE), WIDE)
            held = bt[:, :, cols].reshape(NQ * BLK, WIDE)
            total = jnp.dot(wm[:m], held, preferred_element_type=jnp.float32)
            dst[q, :, rows, cols] += total.reshape(8, rows.size, WIDE)

    swaps = []
    for t, (q, rows) in enumerate(CHUNKS):
        swaps.append(remote(p_out.at[q, :, rows], p_in.at[q, :, rows], cs.at[t], cr.at[t], (z, c, 1 - k)))

    def outer(t):
        ladder(t, 1 - k, p_out)
        add_hole(t, 1 - k, p_out)
        swaps[t].start()

    def inner(t):
        ladder(t, k, p_own)
        add_hole(t, k, p_own)

    def partial(t, owner):
        q, rows = CHUNKS[t]
        return p_own[q, owner, rows] + p_in[q, owner, rows]

    def post(t, i, total):
        n = CHUNKS[t][1].size
        coded, step = encode(total)
        sbuf[t, i, :n, :NA] = coded
        sbuf[t, i, :n, NA:] = step

    def letter(t, i, to):
        n = CHUNKS[t][1].size
        return remote(sbuf.at[t, i, :n], rbuf.at[t, i, :n], zs.at[t, i], zr.at[t, i], (to, c, k))

    def read(t, i):
        n = CHUNKS[t][1].size
        letter(t, i, (z + 1) % 8).wait_recv()
        return decode(rbuf[t, i, :n, :NA], rbuf[t, i, :n, NA:])

    def send_along(t, i, d, total):
        post(t, i, total)
        letter(t, i, (z + d + 8) % 8).start()

    def mine(t, d):
        return partial(t, (z + d + 8) % 8)

    def hops(t, way):
        return 4 if (t + way) % 2 == 0 else 3

    def chain(t, h):
        for way, d in ((0, 1), (1, -1)):
            n = hops(t, way)
            if h < n:
                total = mine(t, d * (n - h))
                if h > 0:
                    total += read(t, way * 4 + h - 1)
                send_along(t, way * 4 + h, d, total)

    def first_round(t):
        send_along(t, 4, -2 if t % 2 == 0 else 2, mine(t, 4))
        send_along(t, 1, 1, mine(t, 3))
        send_along(t, 2, -1, mine(t, -3))
        send_along(t, 0, 1, mine(t, -1))
        send_along(t, 3, -1, mine(t, 1))

    def second_round(t):
        down = mine(t, -2) + read(t, 0) + read(t, 2)
        up = mine(t, 2) + read(t, 1) + read(t, 3)
        if t % 2 == 0:
            send_along(t, 6, 2, up)
            send_along(t, 5, -2, down + read(t, 4))
        else:
            send_along(t, 5, -2, down)
            send_along(t, 6, 2, up + read(t, 4))

    def final(t):
        q, rows = CHUNKS[t]
        if t < CHAINED:
            total = mine(t, 0) + read(t, hops(t, 0) - 1) + read(t, 4 + hops(t, 1) - 1)
        else:
            total = mine(t, 0) + read(t, 5) + read(t, 6)
        total = total / dvm[q, rows]
        lanes = lax.broadcasted_iota(jnp.int32, (rows.size, NA), 1)
        out[q, rows] = jnp.where(c * NA + lanes < limits[q], total, 0.0).astype(jnp.bfloat16)

    def reduce(t):
        swaps[t].wait()
        if t < CHAINED:
            chain(t, 0)
        else:
            first_round(t)

    wait(firsts[0])
    start(seconds[0])
    at_start(0)
    w_wait()
    start(w_first)
    for q in range(1, NQ):
        wait(firsts[q])
        at_start(q)
    start(seconds[1])
    wait(seconds[0])
    start(thirds[0])
    wait(w_first)
    start(w_second)
    start(seconds[2])
    wait(seconds[1])
    start(thirds[1])
    start(seconds[3])
    start(seconds[4])
    for load in loads[1:]:
        load.wait()
    wait(thirds[0])
    ladder(0, 1 - k, p_out)
    ladder(0, k, p_own)
    wait(w_second)
    for q in range(NQ):
        at_wait(q)
        mask_bt(q)
    add_hole(0, 1 - k, p_out)
    swaps[0].start()
    add_hole(0, k, p_own)
    wait(seconds[2])
    start(thirds[2])
    wait(thirds[1])
    outer(1)
    reduce(0)
    inner(1)
    wait(seconds[3])
    start(thirds[3])
    wait(seconds[4])
    start(thirds[4])
    reduce(1)
    wait(thirds[2])
    outer(2)
    chain(0, 1)
    inner(2)
    reduce(2)
    chain(1, 1)
    chain(0, 2)
    wait(thirds[3])
    outer(3)
    inner(3)
    chain(2, 1)
    chain(1, 2)
    wait(thirds[4])
    outer(4)
    reduce(3)
    chain(0, 3)
    inner(4)
    reduce(4)
    chain(2, 2)
    chain(1, 3)
    second_round(3)
    final(0)
    chain(2, 3)
    second_round(4)
    final(1)
    final(3)
    final(2)
    final(4)

    for t in range(NT):
        used = range(7) if t >= CHAINED else [w * 4 + h for w in (0, 1) for h in range(hops(t, w))]
        for i in used:
            letter(t, i, (z + 1) % 8).wait_send()


def per_device(amplitudes, ladder_integrals, hole_integrals, denominators, pair_irrep, irrep_pairs):
    hole = hole_integrals.reshape(NQ, BLK, NQ * BLK)
    anywhere = pl.BlockSpec(memory_space=pl.ANY)
    smem = pl.BlockSpec(memory_space=pltpu.SMEM)
    bf16, f32 = jnp.bfloat16, jnp.float32
    dma = pltpu.SemaphoreType.DMA
    return pl.pallas_call(
        kernel,
        out_shape=jax.ShapeDtypeStruct((NQ, BLK, NA), bf16),
        in_specs=[smem, smem, anywhere, anywhere, anywhere, anywhere],
        out_specs=pl.BlockSpec(memory_space=pltpu.VMEM),
        scratch_shapes=[
            pltpu.VMEM((NQ, KC, NA), bf16),
            pltpu.VMEM((NQ, 4, 2, 2, BLK, KC), bf16),
            pltpu.VMEM((4, 2, 2, NQ, BLK, 128), bf16),
            pltpu.VMEM((NQ, BLK, NA), bf16),
            pltpu.VMEM((NQ, BLK, NA), f32),
            pltpu.VMEM((8 * BLK, KC), bf16),
            pltpu.VMEM((8 * BLK, 128), bf16),
            pltpu.VMEM((NQ, 8, BLK, NA), f32),
            pltpu.VMEM((NQ, 8, BLK, NA), f32),
            pltpu.VMEM((NQ, 8, BLK, NA), f32),
            pltpu.VMEM((NT, 8, BLK, MSG), jnp.int16),
            pltpu.VMEM((NT, 8, BLK, MSG), jnp.int16),
            dma((6,)),
            dma((NQ, 2, 3)), dma((NQ, 2, 3)), dma((NT, 2, 2)), dma((NT, 2, 2)), dma((NT, 4)), dma((NT, 4)),
            dma, dma,
            dma((2, 3)), dma((2, 3)), dma((2, 3)), dma((2, 3)),
            dma((NQ, 2)), dma((NQ, 2)),
            dma((NT,)), dma((NT,)),
            dma((NT, 8)), dma((NT, 8)),
        ],
        compiler_params=pltpu.CompilerParams(
            collective_id=0, has_side_effects=True, vmem_limit_bytes=60 * 1024 * 1024),
    )(pair_irrep, irrep_pairs, amplitudes, ladder_integrals, hole, denominators)


def solution(mesh):
    return jax.shard_map(
        per_device,
        mesh=mesh,
        in_specs=(
            P(None, "col", ("row", "rep")),
            P(None, ("row", "rep"), "col"),
            P(None, ("row", "rep"), None, "col"),
            P(None, ("row", "rep"), "col"),
            P(),
            P(),
        ),
        out_specs=P(None, ("row", "rep"), "col"),
        check_vma=False,
    )
```
